32 devices in a mesh: seq: 4 (over z), vocab: 8 (over y, x, core).
Axes of the slice: x: 2, y: 2, z: 4, core: 2. Of those that a mesh axis runs over, the one named last changes fastest.
Arguments:
- hidden: bfloat16 [2048, 5376], P('seq', 'vocab'), may hold values from -64 to 64
- embed_cotangent: bfloat16 [2048, 5376], P('seq', 'vocab'), may hold values from -24 to 24
- table: bfloat16 [6144, 5376], P('vocab'), may hold values from -3 to 3
- token_ids: int32 [2048], P('seq'), may hold values from 0 to 6143
- target_ids: int32 [2048], P('seq'), may hold values from 0 to 6143
- loss_scale: float32 [2048], P('seq'), may hold values from 8 to 32
Outputs:
- grad_hidden: bfloat16 [2048, 5376], P('seq', 'vocab')
- grad_table: float32 [6144, 5376], P('vocab', 'seq')
- token_loss: float32 [2048], P('seq')
The draws below stay inside these ranges and needn't reach their ends.
All inputs are finite; a program needn't handle non-finite values.
Results may differ from the reference program's by a relative error of at most 0.0047.
Values may be sent and summed in bfloat16 or wider, within the bound.
A program may use at most 192 MiB of HBM per device.

```python
import math
import jax
import jax.numpy as jnp
import numpy as np
from jax import lax

D = 5376
VOCAB = 6144
TOKENS = 2048


def shared_table(key):
    spread = 3.3 / D ** 0.5
    entries = jax.random.normal(jax.random.fold_in(key, 7), (VOCAB, D), jnp.float32)
    return jnp.clip(entries, -6.0, 6.0) * spread


def draw_table(key, part):
    return shared_table(key).astype(jnp.bfloat16)


def draw_hidden(key, part):
    drawn_key = jax.random.fold_in(key, 11)
    entries = jnp.clip(jax.random.normal(drawn_key, (TOKENS, D), jnp.float32), -6.0, 6.0)
    return entries.astype(jnp.bfloat16)


def plant(values, own_key, least, largest):
    spot = [jax.random.randint(jax.random.fold_in(own_key, axis), (), 0, length) for axis, length in enumerate(values.shape)]
    longest = values.shape.index(max(values.shape))
    beside = spot[:longest] + [(spot[longest] + 1) % values.shape[longest]] + spot[longest + 1:]
    return values.at[tuple(spot)].set(least).at[tuple(beside)].set(largest)


def steps_of(rng, shape, shards, smallest, high):
    loudness, own = 1.0, jax.random.fold_in(rng, 6)
    for position, blocks in shards:
        steps = jnp.exp(jax.random.uniform(jax.random.fold_in(own, position), (blocks,), jnp.float32, smallest / len(shards), high / len(shards)))
        loudness = loudness * jnp.repeat(steps, shape[position] // blocks).reshape([-1 if axis == position else 1 for axis in range(len(shape))])
    return loudness


def cumulative_ranks(number_of, lean):
    portions = [(1 << 20) // math.isqrt(standing ** lean) + 1 for standing in range(1, number_of + 1)]
    scale = 1 + sum(portions) // (1 << 30)
    return np.cumsum(np.array([max(1, weight // scale) for weight in portions]))


def ranked(key, shape, amount, lean):
    listing = cumulative_ranks(amount, lean)
    ticket = jax.random.randint(jax.random.fold_in(key, 1), shape, 0, int(listing[amount - 1]))
    standing = jnp.searchsorted(jnp.asarray(listing, jnp.int32), ticket, side="right")
    return jax.random.permutation(jax.random.fold_in(key, 2), amount)[standing].astype(jnp.int32)


def normal_values(key, extent, scale, most, cuts=(), kind=jnp.bfloat16):
    values = jax.random.normal(key, extent, jnp.float32) * scale
    if len(cuts) > 0:
        values = steps_of(key, extent, cuts, -0.22, 0.18) * values
    return jnp.clip(values, min=-most, max=most).astype(kind)


def setup_inputs(seed: int = 0) -> dict:
    streams_of = jax.random.split(jax.random.key(seed), 7)
    return {
        "hidden": draw_hidden(jax.random.fold_in(streams_of[6], 71), 0),
        "embed_cotangent": normal_values(streams_of[1], (TOKENS, D), 4.0, 24.0, ((0, 4), (1, 8))),
        "table": draw_table(jax.random.fold_in(streams_of[6], 71), 0),
        "token_ids": plant(ranked(streams_of[3], (TOKENS,), VOCAB, 2), jax.random.fold_in(streams_of[3], 3), 0, VOCAB - 1).astype(jnp.int32),
        "target_ids": plant(jax.random.randint(streams_of[4], (TOKENS,), 0, VOCAB), jax.random.fold_in(streams_of[4], 1), 0, VOCAB - 1).astype(jnp.int32),
        "loss_scale": jnp.clip(jnp.exp(math.log(32.0) - 1.3862944 * jax.random.uniform(streams_of[5], (TOKENS,), jnp.float32) ** steps_of(streams_of[5], (TOKENS,), ((0, 4),), -0.2, 0.2)), 8.0, 32.0),
    }


def reference(hidden, embed_cotangent, table, token_ids, target_ids, loss_scale):
    logits = lax.dot_general(hidden, table, (((1,), (1,)), ((), ())), preferred_element_type=jnp.float32)
    vocab_ids = jnp.arange(table.shape[0], dtype=jnp.int32)
    target_hot = (target_ids[:, None] == vocab_ids[None, :]).astype(jnp.float32)
    row_top = jnp.max(logits, axis=1)
    exp_total = jnp.sum(jnp.exp(logits - row_top[:, None]), axis=1)
    target_logit = jnp.sum(logits * target_hot, axis=1)
    log_norm = row_top + jnp.log(exp_total)
    token_loss = log_norm - target_logit
    probability = jnp.exp(logits - log_norm[:, None])
    logit_grad = (loss_scale[:, None] * (probability - target_hot)).astype(jnp.bfloat16)
    grad_hidden = jnp.dot(logit_grad, table, preferred_element_type=jnp.float32).astype(jnp.bfloat16)
    head_part = lax.dot_general(logit_grad, hidden, (((0,), (0,)), ((), ())), preferred_element_type=jnp.float32)
    embed_part = jax.ops.segment_sum(embed_cotangent.astype(jnp.float32), token_ids, num_segments=table.shape[0])
    grad_table = head_part + embed_part
    return (grad_hidden, grad_table, token_loss)
```

```python
import jax
import jax.numpy as jnp
from jax import lax
from jax.sharding import PartitionSpec as P


def body(hidden, embed_cotangent, table, token_ids, target_ids, loss_scale):
    n_seq, n_vocab = lax.axis_size("seq"), lax.axis_size("vocab")
    per = n_vocab // n_seq
    vocab_rows = table.shape[0]
    vocab_base = lax.axis_index("vocab") * vocab_rows
    columns = vocab_base + jnp.arange(vocab_rows, dtype=jnp.int32)
    rows_full = lax.all_gather(hidden, "vocab", axis=1, tiled=True)
    swap = [
        (s * n_vocab + c * per + r, c * n_vocab + s * per + r)
        for s in range(n_seq)
        for c in range(n_seq)
        for r in range(per)
    ]
    hidden_cols = lax.all_gather(lax.ppermute(hidden, ("seq", "vocab"), swap), "vocab", axis=0)
    cot_cols = lax.all_gather(
        lax.ppermute(embed_cotangent, ("seq", "vocab"), swap), "vocab", axis=0
    )
    ids_all = lax.all_gather(token_ids, "seq", axis=0, tiled=True)
    logits = lax.dot_general(
        rows_full, table, (((1,), (1,)), ((), ())), preferred_element_type=jnp.float32
    )
    target_hot = (target_ids[:, None] == columns[None, :]).astype(jnp.float32)
    own_top = jnp.max(logits, axis=1)
    own_total = jnp.sum(jnp.exp(logits - own_top[:, None]), axis=1)
    own_target = jnp.sum(logits * target_hot, axis=1)
    stats = lax.all_gather(jnp.stack([own_top, own_total, own_target]), "vocab", axis=0)
    row_top = jnp.max(stats[:, 0], axis=0)
    exp_total = jnp.sum(stats[:, 1] * jnp.exp(stats[:, 0] - row_top), axis=0)
    log_norm = row_top + jnp.log(exp_total)
    token_loss = log_norm - jnp.sum(stats[:, 2], axis=0)
    probability = jnp.exp(logits - log_norm[:, None])
    logit_grad = (loss_scale[:, None] * (probability - target_hot)).astype(jnp.bfloat16)
    grad_all = lax.all_gather(logit_grad, "seq", axis=0)
    hidden_term = jnp.dot(logit_grad, table, preferred_element_type=jnp.float32)
    grad_hidden = lax.psum_scatter(
        hidden_term.astype(jnp.bfloat16), "vocab", scatter_dimension=1, tiled=True
    )
    rows, cols = hidden.shape

    def columns_of(blocks):
        blocks = blocks.reshape(n_seq, per, rows, cols).transpose(0, 2, 1, 3)
        return blocks.reshape(n_seq * rows, per * cols)

    contract_rows = (((0,), (0,)), ((), ()))
    token_hot = (ids_all[:, None] == columns[None, :]).astype(jnp.bfloat16)
    grad_table = lax.dot_general(
        token_hot, columns_of(cot_cols), contract_rows, preferred_element_type=jnp.float32
    ) + lax.dot_general(
        grad_all.reshape(n_seq * rows, vocab_rows),
        columns_of(hidden_cols),
        contract_rows,
        preferred_element_type=jnp.float32,
    )
    return (grad_hidden, grad_table, token_loss)


def solution(mesh):
    placed = (P("seq", "vocab"), P("seq", "vocab"), P("vocab", None), P("seq"), P("seq"), P("seq"))
    return jax.shard_map(
        body,
        mesh=mesh,
        in_specs=placed,
        out_specs=(P("seq", "vocab"), P("vocab", "seq"), P("seq")),
        check_vma=False,
    )
```

```python
import functools

import jax
import jax.numpy as jnp
from jax import lax
from jax.experimental import pallas as pl
from jax.experimental.pallas import tpu as pltpu
from jax.sharding import PartitionSpec as P

MESH = pl.DeviceIdType.MESH
F32 = jnp.float32
BF16 = jnp.bfloat16
CORES = 2
CHUNK = 128


def dot(a, b, dims=(((1,), (0,)), ((), ()))):
    return lax.dot_general(a, b, dims, preferred_element_type=F32)


def kernel(
    n_seq, n_vocab,
    hid, cot, table, ids, target, scale,
    gh, gt, loss,
    raw, tab, rows, hcols, ccols, grads, logits, sends, sib, shares, own, stats, ids_all, norm,
    table_sem, local_sem, push_sem, fwd_sem, block_sem, swap_sem, stat_send, stat_recv, ids_send, ids_recv,
    up_sem, down_sem, grads_recv, sib_send, sib_recv, share_send, share_recv,
):
    per = n_vocab // n_seq
    chips = n_vocab // CORES
    cols, tokens = hid.shape
    vocab_rows, _ = table.shape
    s, v = lax.axis_index("seq"), lax.axis_index("vocab")
    c, k = v // CORES, v % CORES
    twin = c * CORES + (1 - k)
    swap_to, swap_slot = v // per, s * per + v % per
    is_self = swap_to == s
    base = v * vocab_rows

    def remote(src, dst, send, recv, where):
        return pltpu.make_async_remote_copy(
            src_ref=src, dst_ref=dst, send_sem=send, recv_sem=recv,
            device_id=where, device_id_type=MESH,
        )

    def loop(lo, hi, fn):
        lax.fori_loop(lo, hi, lambda i, z: (fn(i), z)[1], 0)

    def fetch(i):
        at = pl.ds(pl.multiple_of(i * CHUNK, CHUNK), CHUNK)
        return pltpu.make_async_copy(table.at[at], raw.at[i % 2], table_sem.at[i % 2])
    fetch(0).start()
    keep = pltpu.make_async_copy(hid, rows.at[v], local_sem)
    keep.start()

    barrier = pltpu.get_barrier_semaphore()
    loop(1, n_vocab, lambda i: pl.semaphore_signal(
        barrier, inc=1, device_id=(s, (v + i) % n_vocab), device_id_type=MESH))
    loop(1, n_seq, lambda i: pl.semaphore_signal(
        barrier, inc=1, device_id=((s + i) % n_seq, v), device_id_type=MESH))

    @pl.when(jnp.logical_not(is_self))
    def _():
        pl.semaphore_signal(barrier, inc=1, device_id=(swap_to, swap_slot), device_id_type=MESH)

    pl.semaphore_wait(barrier, n_vocab + n_seq - 2 + jnp.where(is_self, 0, 1))

    def push(a, src, buf):
        def one(i):
            return remote(src, buf.at[v], push_sem.at[a, i], block_sem.at[a, v],
                          (s, ((c + i) % chips) * CORES + k))
        loop(1, chips, lambda i: one(i).start())
        remote(src, buf.at[v], push_sem.at[a, 0], block_sem.at[a, v], (s, twin)).start()

    def push_done(a, src, buf):
        def one(i):
            remote(src, buf.at[v], push_sem.at[a, i], block_sem.at[a, v], (s, twin)).wait_send()
        loop(0, chips, one)

    def arrived(a, buf, u):
        remote(buf.at[u], buf.at[u], fwd_sem.at[a, 0], block_sem.at[a, u], (s, twin)).wait_recv()

    def forward(a, buf, i):
        u = ((c + i) % chips) * CORES + k
        return remote(buf.at[u], buf.at[u], fwd_sem.at[a, i], block_sem.at[a, u], (s, twin))

    push(0, hid, rows)

    for a, src, buf in ((1, hid, hcols), (2, cot, ccols)):
        @pl.when(is_self)
        def _(a=a, src=src, buf=buf):
            stay = pltpu.make_async_copy(src, buf.at[v], swap_sem.at[a])
            stay.start()
            stay.wait()

        @pl.when(jnp.logical_not(is_self))
        def _(a=a, src=src, buf=buf):
            remote(src, buf.at[swap_slot], swap_sem.at[a], block_sem.at[a, swap_slot],
                   (swap_to, swap_slot)).start()

    ids_all[s] = ids[...]

    def send_ids(i):
        remote(ids, ids_all.at[s], ids_send.at[i], ids_recv.at[s], ((s + i) % n_seq, v)).start()
    loop(1, n_seq, send_ids)

    pieces = vocab_rows // CHUNK

    def split(i):
        @pl.when(i + 1 < pieces)
        def _():
            fetch(i + 1).start()
        fetch(i).wait()
        at = pl.ds(pl.multiple_of(i * CHUNK, CHUNK), CHUNK)
        for u in range(n_vocab):
            tab[u, at, :] = raw[i % 2, :, u * cols:(u + 1) * cols]
    loop(0, pieces, split)

    logits[...] = jnp.zeros_like(logits)
    gt[...] = jnp.zeros_like(gt)
    keep.wait()

    def add_logits(u):
        logits[...] += dot(tab[u], rows[u])

    def logit_step(i):
        ci = (c + i) % chips

        @pl.when(i > 0)
        def _():
            arrived(0, rows, ci * CORES + k)
            forward(0, rows, i).start()
        add_logits(ci * CORES + k)
        arrived(0, rows, ci * CORES + 1 - k)
        add_logits(ci * CORES + 1 - k)
    loop(0, chips, logit_step)

    @pl.when(jnp.logical_not(is_self))
    def _():
        arrived(1, hcols, v)
        arrived(2, ccols, v)
    push(1, hcols.at[v], hcols)

    def piece(i):
        at = pl.ds(pl.multiple_of(i * CHUNK, CHUNK), CHUNK)
        entry = base + i * CHUNK + lax.broadcasted_iota(jnp.int32, (CHUNK, tokens), 0)
        return at, entry

    top = lax.fori_loop(
        0, pieces,
        lambda i, m: jnp.maximum(m, jnp.max(logits[piece(i)[0], :], axis=0, keepdims=True)),
        jnp.full((1, tokens), -jnp.inf, F32))

    def sums(i, carry):
        total, picked = carry
        at, entry = piece(i)
        x = logits[at, :]
        total += jnp.sum(jnp.exp(x - top), axis=0, keepdims=True)
        picked += jnp.sum(jnp.where(entry == target[...], x, 0.0), axis=0, keepdims=True)
        return total, picked
    zero = jnp.zeros((1, tokens), F32)
    total, picked = lax.fori_loop(0, pieces, sums, (zero, zero))
    stats[v] = jnp.concatenate([top, total, picked, jnp.zeros((5, tokens), F32)], axis=0)

    def stat(i):
        return remote(stats.at[v], stats.at[v], stat_send.at[i], stat_recv.at[v],
                      (s, (v + i) % n_vocab))
    loop(1, n_vocab, lambda i: stat(i).start())

    def stat_wait(i):
        u = (v + i) % n_vocab
        remote(stats.at[u], stats.at[u], stat_send.at[i], stat_recv.at[u], (s, twin)).wait_recv()
    loop(1, n_vocab, stat_wait)
    every = stats[...]
    row_top = jnp.max(every[:, 0, :], axis=0, keepdims=True)
    exp_total = jnp.sum(every[:, 1, :] * jnp.exp(every[:, 0, :] - row_top), axis=0, keepdims=True)
    log_norm = row_top + jnp.log(exp_total)
    loss[...] = log_norm - jnp.sum(every[:, 2, :], axis=0, keepdims=True)
    norm[...] = log_norm

    def logit_grad(i):
        at, entry = piece(i)
        hot = jnp.where(entry == target[...], 1.0, 0.0)
        g = scale[...] * (jnp.exp(logits[at, :] - norm[...]) - hot)
        grads[s, :, at] = g.T.astype(BF16)
    loop(0, pieces, logit_grad)

    def go_up(b):
        return remote(grads.at[b], grads.at[b], up_sem.at[b], grads_recv.at[b],
                      (jnp.minimum(s + 1, n_seq - 1), v))

    def go_down(b):
        return remote(grads.at[b], grads.at[b], down_sem.at[b], grads_recv.at[b],
                      (jnp.maximum(s - 1, 0), v))

    @pl.when(s < n_seq - 1)
    def _():
        go_up(s).start()

    @pl.when(s > 0)
    def _():
        go_down(s).start()

    def sib_copy(ci):
        slot = sends.at[ci * CORES + 1 - k]
        return remote(slot, sib.at[ci], sib_send.at[ci], sib_recv.at[ci], (s, twin))

    def to_twin(i):
        ci = (c + i) % chips
        u = ci * CORES + 1 - k
        sends[u] = dot(grads[s], tab[u]).astype(BF16)
        sib_copy(ci).start()
    loop(1, chips + 1, to_twin)

    def share_copy(ci):
        slot = sends.at[ci * CORES + k]
        return remote(slot, shares.at[c], share_send.at[ci], share_recv.at[c], (s, ci * CORES + k))

    def to_chips(i):
        ci = (c + i) % chips
        u = ci * CORES + k
        own[...] = dot(grads[s], tab[u])
        sib_copy(ci).wait_recv()
        own[...] += sib[ci].astype(F32)

        @pl.when(i < chips)
        def _():
            sends[u] = own[...].astype(BF16)
            share_copy(ci).start()
    loop(1, chips + 1, to_chips)
    push(2, ccols.at[v], ccols)

    def add_head(b):
        def one(r):
            gt[r] += dot(hcols[b * per + r], grads[b])
        loop(0, per, one)

    def take_grads(j):
        @pl.when(s >= j)
        def _():
            b = s - j
            go_up(b).wait_recv()

            @pl.when(s < n_seq - 1)
            def _():
                go_up(b).start()

        @pl.when(s + j < n_seq)
        def _():
            b = s + j
            go_down(b).wait_recv()

            @pl.when(s > 0)
            def _():
                go_down(b).start()

    def add_heads(j):
        @pl.when(s >= j)
        def _():
            add_head(s - j)

        @pl.when(s + j < n_seq)
        def _():
            add_head(s + j)

    def relay(a, buf):
        def one(i):
            arrived(a, buf, ((c + i) % chips) * CORES + k)
            forward(a, buf, i).start()
        loop(1, chips, one)
        loop(0, chips, lambda i: arrived(a, buf, ((c + i) % chips) * CORES + 1 - k))

    take_grads(1)
    relay(1, hcols)
    add_head(s)
    add_heads(1)
    for j in range(2, n_seq):
        take_grads(j)
        add_heads(j)

    def ids_wait(i):
        b = (s + i) % n_seq
        remote(ids, ids_all.at[b], ids_send.at[i], ids_recv.at[b], ((s + i) % n_seq, v)).wait_recv()
    loop(1, n_seq, ids_wait)

    def share_add(i):
        ci = (c + i) % chips
        remote(shares.at[ci], shares.at[ci], share_send.at[ci], share_recv.at[ci],
               (s, twin)).wait_recv()
        own[...] += shares[ci].astype(F32)
    loop(1, chips, share_add)
    gh[...] = own[...].T.astype(BF16)

    relay(2, ccols)

    def add_embed(b):
        entry = base + lax.broadcasted_iota(jnp.int32, (vocab_rows, tokens), 0)
        hot = jnp.where(entry == ids_all[b][0:1, :], 1.0, 0.0).astype(BF16)

        def one(r):
            gt[r] += dot(ccols[b * per + r], hot, (((1,), (1,)), ((), ())))
        loop(0, per, one)
    loop(0, n_seq, add_embed)

    push_done(0, hid, rows)
    push_done(1, hcols.at[v], hcols)
    push_done(2, ccols.at[v], ccols)
    for a, buf in ((0, rows), (1, hcols), (2, ccols)):
        loop(1, chips, lambda i, a=a, buf=buf: forward(a, buf, i).wait_send())
    for a, src, buf in ((1, hid, hcols), (2, cot, ccols)):
        @pl.when(jnp.logical_not(is_self))
        def _(a=a, src=src, buf=buf):
            remote(src, buf.at[swap_slot], swap_sem.at[a], block_sem.at[a, swap_slot],
                   (swap_to, swap_slot)).wait_send()

    def ids_left(i):
        remote(ids, ids_all.at[s], ids_send.at[i], ids_recv.at[s], ((s + i) % n_seq, v)).wait_send()
    loop(1, n_seq, ids_left)
    loop(1, n_vocab, lambda i: stat(i).wait_send())
    loop(0, chips, lambda i: sib_copy(i).wait_send())
    loop(1, chips, lambda i: share_copy((c + i) % chips).wait_send())
    for b in range(n_seq):
        @pl.when(jnp.logical_and(s >= b, s < n_seq - 1))
        def _(b=b):
            go_up(b).wait_send()

        @pl.when(jnp.logical_and(s <= b, s > 0))
        def _(b=b):
            go_down(b).wait_send()


def body(hidden, embed_cotangent, table, token_ids, target_ids, loss_scale):
    n_seq, n_vocab = lax.axis_size("seq"), lax.axis_size("vocab")
    per, chips = n_vocab // n_seq, n_vocab // CORES
    tokens, cols = hidden.shape
    vocab_rows, width = table.shape
    vmem = pl.BlockSpec(memory_space=pltpu.VMEM)
    dma = pltpu.SemaphoreType.DMA
    blocks = pltpu.VMEM((n_vocab, cols, tokens), BF16)
    halves = pltpu.VMEM((chips, tokens, cols), BF16)
    gh, gt, loss = pl.pallas_call(
        functools.partial(kernel, n_seq, n_vocab),
        out_shape=(
            jax.ShapeDtypeStruct((cols, tokens), BF16),
            jax.ShapeDtypeStruct((per, cols, vocab_rows), F32),
            jax.ShapeDtypeStruct((1, tokens), F32),
        ),
        in_specs=[vmem, vmem, pl.BlockSpec(memory_space=pl.ANY), vmem, vmem, vmem],
        out_specs=(vmem, vmem, vmem),
        scratch_shapes=[
            pltpu.VMEM((2, CHUNK, width), BF16),
            pltpu.VMEM((n_vocab, vocab_rows, cols), BF16),
            blocks, blocks, blocks,
            pltpu.VMEM((n_seq, tokens, vocab_rows), BF16),
            pltpu.VMEM((vocab_rows, tokens), F32),
            pltpu.VMEM((n_vocab, tokens, cols), BF16),
            halves, halves,
            pltpu.VMEM((tokens, cols), F32),
            pltpu.VMEM((n_vocab, 8, tokens), F32),
            pltpu.VMEM((n_seq, 8, tokens), jnp.int32),
            pltpu.VMEM((1, tokens), F32),
            dma((2,)), dma,
            dma((3, chips)), dma((3, chips)), dma((3, n_vocab)), dma((3,)),
            dma((n_vocab,)), dma((n_vocab,)), dma((n_seq,)), dma((n_seq,)),
            dma((n_seq,)), dma((n_seq,)), dma((n_seq,)),
            dma((chips,)), dma((chips,)), dma((chips,)), dma((chips,)),
        ],
        compiler_params=pltpu.CompilerParams(
            collective_id=0, has_side_effects=True, vmem_limit_bytes=62 * 1024 * 1024
        ),
        cost_estimate=pl.CostEstimate(
            flops=8 * tokens * vocab_rows * width, bytes_accessed=2 * vocab_rows * width,
            transcendentals=2 * tokens * vocab_rows,
        ),
    )(
        hidden.T, embed_cotangent.T, table,
        jnp.broadcast_to(token_ids[None, :], (8, tokens)),
        target_ids[None, :], loss_scale[None, :],
    )
    return (gh.T, gt.reshape(per * cols, vocab_rows).T, loss[0])


def solution(mesh):
    placed = (P("seq", "vocab"), P("seq", "vocab"), P("vocab", None), P("seq"), P("seq"), P("seq"))
    return jax.shard_map(
        body,
        mesh=mesh,
        in_specs=placed,
        out_specs=(P("seq", "vocab"), P("vocab", "seq"), P("seq")),
        check_vma=False,
    )
```

```python
import functools

import jax
import jax.numpy as jnp
from jax import lax
from jax.experimental import pallas as pl
from jax.experimental.pallas import tpu as pltpu
from jax.sharding import PartitionSpec as P

MESH = pl.DeviceIdType.MESH
F32 = jnp.float32
BF16 = jnp.bfloat16
CORES = 2
CHUNK = 128


def dot(a, b, dims=(((1,), (0,)), ((), ()))):
    return lax.dot_general(a, b, dims, preferred_element_type=F32)


def kernel(
    n_seq, n_vocab,
    hid, cot, table, ids, target, scale,
    gh, gt, loss,
    raw, tab, rows, hcols, ccols, grads, logits, sends, sib, shares, own, stats, ids_all, norm, stage,
    table_sem, local_sem, push_sem, fwd_sem, block_sem, half_send, half_recv,
    stage_send, stage_recv, cross_send, cross_recv, stat_send, stat_recv, ids_send, ids_recv,
    up_sem, down_sem, grads_recv, sib_send, sib_recv, share_send, share_recv,
):
    per = n_vocab // n_seq
    chips = n_vocab // CORES
    cols, tokens = hid.shape
    vocab_rows, _ = table.shape
    s, v = lax.axis_index("seq"), lax.axis_index("vocab")
    c, k = v // CORES, v % CORES
    twin = c * CORES + (1 - k)
    q, r = v // per, v % per
    quarter = tokens // n_seq
    square = chips == 4
    nx, ny, nd = c + 1 - 2 * (c % 2), (c + 2) % 4, 3 - c
    half = cols // 2
    base = v * vocab_rows

    def remote(src, dst, send, recv, where):
        return pltpu.make_async_remote_copy(
            src_ref=src, dst_ref=dst, send_sem=send, recv_sem=recv,
            device_id=where, device_id_type=MESH,
        )

    def lanes(b):
        return pl.ds(pl.multiple_of(b * quarter, quarter), quarter)

    def loop(lo, hi, fn):
        lax.fori_loop(lo, hi, lambda i, z: (fn(i), z)[1], 0)

    def fetch(i):
        at = pl.ds(pl.multiple_of(i * CHUNK, CHUNK), CHUNK)
        return pltpu.make_async_copy(table.at[at], raw.at[i % 2], table_sem.at[i % 2])
    fetch(0).start()
    keep = pltpu.make_async_copy(hid, rows.at[v], local_sem)
    keep.start()

    barrier = pltpu.get_barrier_semaphore()
    loop(1, n_vocab, lambda i: pl.semaphore_signal(
        barrier, inc=1, device_id=(s, (v + i) % n_vocab), device_id_type=MESH))
    loop(1, n_seq, lambda i: pl.semaphore_signal(
        barrier, inc=1, device_id=((s + i) % n_seq, v), device_id_type=MESH))

    pl.semaphore_wait(barrier, n_vocab + n_seq - 2)

    def core_of(chip, core):
        return chip * CORES + core

    def peers(fn):
        if square:
            fn(1, nx)
            fn(2, ny)
        else:
            loop(1, chips, lambda i: fn(i, (c + i) % chips))

    def push_copy(a, src, buf, i, u):
        return remote(src, buf.at[v], push_sem.at[a, i], block_sem.at[a, v], (s, u))

    def push(a, src, buf):
        peers(lambda i, chip: push_copy(a, src, buf, i, core_of(chip, k)).start())
        push_copy(a, src, buf, 0, twin).start()

    def arrived(a, buf, u):
        remote(buf.at[u], buf.at[u], fwd_sem.at[a, 0], block_sem.at[a, u], (s, twin)).wait_recv()

    def forward(a, buf, i, u):
        return remote(buf.at[u], buf.at[u], fwd_sem.at[a, i], block_sem.at[a, u], (s, twin))

    def half_copy(a, buf, i, u, chip):
        part = buf.at[u, pl.ds(i * half, half), :]
        return remote(part, part, half_send.at[a, i], half_recv.at[a, i], (s, core_of(chip, k)))

    def near(a, buf):
        def one(i, chip):
            u = core_of(chip, k)
            arrived(a, buf, u)
            if square:
                half_copy(a, buf, i - 1, u, ny if i == 1 else nx).start()
            forward(a, buf, i, u).start()
        peers(one)

    def far(a, buf):
        if square:
            u = core_of(nd, k)
            half_copy(a, buf, 0, u, ny).wait_recv()
            half_copy(a, buf, 1, u, nx).wait_recv()
            forward(a, buf, 3, u).start()

    def from_twin(a, buf):
        loop(0, chips, lambda i: arrived(a, buf, core_of((c + i) % chips, 1 - k)))

    def gather_done(a, src, buf):
        peers(lambda i, chip: push_copy(a, src, buf, i, core_of(chip, k)).wait_send())
        push_copy(a, src, buf, 0, twin).wait_send()
        loop(1, chips, lambda i: forward(a, buf, i, v).wait_send())
        if square:
            half_copy(a, buf, 0, v, ny).wait_send()
            half_copy(a, buf, 1, v, nx).wait_send()

    push(0, hid, rows)

    def stage_copy(to):
        return remote(cot.at[:, lanes(to)], stage.at[q], stage_send.at[to], stage_recv.at[q],
                      (s, to * per + r))
    loop(1, n_seq, lambda j: stage_copy((q + j) % n_seq).start())
    stage[q] = cot[:, lanes(q)]

    def cross(a, j, src, buf):
        d = (s + j) % n_seq
        return remote(src(d), buf.at[v, :, lanes(s)], cross_send.at[a, j], cross_recv.at[a, s], (d, v))

    def cross_in(a, buf):
        def one(j):
            b = (s + j) % n_seq
            here = buf.at[v, :, lanes(b)]
            remote(here, here, cross_send.at[a, j], cross_recv.at[a, b], (b, v)).wait_recv()
        loop(1, n_seq, one)

    def cot_part(d):
        return stage.at[d]

    def hid_part(d):
        return rows.at[d * per + r, :, lanes(q)]

    ids_all[s] = ids[...]

    def send_ids(i):
        remote(ids, ids_all.at[s], ids_send.at[i], ids_recv.at[s], ((s + i) % n_seq, v)).start()
    loop(1, n_seq, send_ids)

    pieces = vocab_rows // CHUNK

    def split(i):
        @pl.when(i + 1 < pieces)
        def _():
            fetch(i + 1).start()
        fetch(i).wait()
        at = pl.ds(pl.multiple_of(i * CHUNK, CHUNK), CHUNK)
        for u in range(n_vocab):
            tab[u, at, :] = raw[i % 2, :, u * cols:(u + 1) * cols]
    loop(0, pieces, split)

    def stage_in(j):
        b = (q + j) % n_seq
        remote(stage.at[b], stage.at[b], stage_send.at[b], stage_recv.at[b], (s, twin)).wait_recv()
    loop(1, n_seq, stage_in)
    loop(1, n_seq, lambda j: cross(1, j, cot_part, ccols).start())
    ccols[v, :, lanes(s)] = stage[s]

    logits[...] = jnp.zeros_like(logits)
    gt[...] = jnp.zeros_like(gt)
    keep.wait()

    def add_logits(u):
        logits[...] += dot(tab[u], rows[u])

    add_logits(v)
    near(0, rows)

    def step(i):
        chip = (c + i) % chips
        mine = core_of(chip, k)

        if not square:
            @pl.when(i > 0)
            def _():
                add_logits(mine)
        arrived(0, rows, core_of(chip, 1 - k))
        add_logits(core_of(chip, 1 - k))
    if square:
        def pair(i):
            chip = nx * (1 - i) + ny * i
            add_logits(core_of(chip, k))
            arrived(0, rows, core_of(chip, 1 - k))
            add_logits(core_of(chip, 1 - k))
        loop(0, 2, pair)
        far(0, rows)
        add_logits(core_of(nd, k))

    loop(1, n_seq, lambda j: cross(0, j, hid_part, hcols).start())
    hcols[v, :, lanes(s)] = rows[s * per + r, :, lanes(q)]
    if square:
        def last(i):
            chip = c * (1 - i) + nd * i
            arrived(0, rows, core_of(chip, 1 - k))
            add_logits(core_of(chip, 1 - k))
        loop(0, 2, last)
    else:
        loop(0, chips, step)

    def piece(i):
        at = pl.ds(pl.multiple_of(i * CHUNK, CHUNK), CHUNK)
        entry = base + i * CHUNK + lax.broadcasted_iota(jnp.int32, (CHUNK, tokens), 0)
        return at, entry

    top = lax.fori_loop(
        0, pieces,
        lambda i, m: jnp.maximum(m, jnp.max(logits[piece(i)[0], :], axis=0, keepdims=True)),
        jnp.full((1, tokens), -jnp.inf, F32))

    def sums(i, carry):
        total, picked = carry
        at, entry = piece(i)
        x = logits[at, :]
        total += jnp.sum(jnp.exp(x - top), axis=0, keepdims=True)
        picked += jnp.sum(jnp.where(entry == target[...], x, 0.0), axis=0, keepdims=True)
        return total, picked
    zero = jnp.zeros((1, tokens), F32)
    total, picked = lax.fori_loop(0, pieces, sums, (zero, zero))
    stats[v] = jnp.concatenate([top, total, picked, jnp.zeros((5, tokens), F32)], axis=0)

    def stat(i):
        return remote(stats.at[v], stats.at[v], stat_send.at[i], stat_recv.at[v],
                      (s, (v + i) % n_vocab))
    loop(1, n_vocab, lambda i: stat(i).start())
    cross_in(1, ccols)
    push(1, ccols.at[v], ccols)

    def stat_wait(i):
        u = (v + i) % n_vocab
        remote(stats.at[u], stats.at[u], stat_send.at[i], stat_recv.at[u], (s, twin)).wait_recv()
    loop(1, n_vocab, stat_wait)
    every = stats[...]
    row_top = jnp.max(every[:, 0, :], axis=0, keepdims=True)
    exp_total = jnp.sum(every[:, 1, :] * jnp.exp(every[:, 0, :] - row_top), axis=0, keepdims=True)
    log_norm = row_top + jnp.log(exp_total)
    loss[...] = log_norm - jnp.sum(every[:, 2, :], axis=0, keepdims=True)
    norm[...] = log_norm

    def logit_grad(i):
        at, entry = piece(i)
        hot = jnp.where(entry == target[...], 1.0, 0.0)
        g = scale[...] * (jnp.exp(logits[at, :] - norm[...]) - hot)
        grads[s, :, at] = g.T.astype(BF16)
    loop(0, pieces, logit_grad)

    def go_up(b):
        return remote(grads.at[b], grads.at[b], up_sem.at[b], grads_recv.at[b],
                      (jnp.minimum(s + 1, n_seq - 1), v))

    def go_down(b):
        return remote(grads.at[b], grads.at[b], down_sem.at[b], grads_recv.at[b],
                      (jnp.maximum(s - 1, 0), v))

    @pl.when(s < n_seq - 1)
    def _():
        go_up(s).start()

    @pl.when(s > 0)
    def _():
        go_down(s).start()

    def sib_copy(ci):
        slot = sends.at[ci * CORES + 1 - k]
        return remote(slot, sib.at[ci], sib_send.at[ci], sib_recv.at[ci], (s, twin))

    def to_twin(i):
        ci = (c + i) % chips
        u = ci * CORES + 1 - k
        sends[u] = dot(grads[s], tab[u]).astype(BF16)
        sib_copy(ci).start()
    loop(1, chips + 1, to_twin)
    near(1, ccols)
    cross_in(0, hcols)
    push(2, hcols.at[v], hcols)

    def share_copy(ci):
        slot = sends.at[ci * CORES + k]
        return remote(slot, shares.at[c], share_send.at[ci], share_recv.at[c], (s, ci * CORES + k))

    def to_chips(i):
        ci = (c + i) % chips
        u = ci * CORES + k
        own[...] = dot(grads[s], tab[u])
        sib_copy(ci).wait_recv()
        own[...] += sib[ci].astype(F32)

        @pl.when(i < chips)
        def _():
            sends[u] = own[...].astype(BF16)
            share_copy(ci).start()
    loop(1, chips + 1, to_chips)

    def tokens_of(buf, b, j):
        return jnp.concatenate([buf[i * per + j, :, lanes(b)] for i in range(n_seq)], axis=1)

    def add_head(b):
        def one(j):
            gt[j] += dot(tokens_of(hcols, b, j), grads[b])
        loop(0, per, one)

    def take_grads(j):
        @pl.when(s >= j)
        def _():
            b = s - j
            go_up(b).wait_recv()

            @pl.when(s < n_seq - 1)
            def _():
                go_up(b).start()

        @pl.when(s + j < n_seq)
        def _():
            b = s + j
            go_down(b).wait_recv()

            @pl.when(s > 0)
            def _():
                go_down(b).start()

    def add_heads(j):
        @pl.when(s >= j)
        def _():
            add_head(s - j)

        @pl.when(s + j < n_seq)
        def _():
            add_head(s + j)

    def ids_wait(i):
        b = (s + i) % n_seq
        remote(ids, ids_all.at[b], ids_send.at[i], ids_recv.at[b], ((s + i) % n_seq, v)).wait_recv()

    def add_embed(b):
        entry = base + lax.broadcasted_iota(jnp.int32, (vocab_rows, tokens), 0)
        hot = jnp.where(entry == ids_all[b][0:1, :], 1.0, 0.0).astype(BF16)

        def one(j):
            gt[j] += dot(tokens_of(ccols, b, j), hot, (((1,), (1,)), ((), ())))
        loop(0, per, one)

    take_grads(1)
    far(1, ccols)
    near(2, hcols)
    loop(1, n_seq, ids_wait)
    from_twin(1, ccols)
    loop(0, n_seq, add_embed)
    if n_seq > 2:
        take_grads(2)
    far(2, hcols)
    from_twin(2, hcols)
    add_head(s)
    add_heads(1)
    for j in range(2, n_seq):
        if j > 2:
            take_grads(j)
        add_heads(j)

    def share_add(i):
        ci = (c + i) % chips
        remote(shares.at[ci], shares.at[ci], share_send.at[ci], share_recv.at[ci],
               (s, twin)).wait_recv()
        own[...] += shares[ci].astype(F32)
    loop(1, chips, share_add)
    gh[...] = own[...].T.astype(BF16)

    gather_done(0, hid, rows)
    gather_done(1, ccols.at[v], ccols)
    gather_done(2, hcols.at[v], hcols)
    loop(1, n_seq, lambda j: stage_copy((q + j) % n_seq).wait_send())
    loop(1, n_seq, lambda j: cross(0, j, hid_part, hcols).wait_send())
    loop(1, n_seq, lambda j: cross(1, j, cot_part, ccols).wait_send())

    def ids_left(i):
        remote(ids, ids_all.at[s], ids_send.at[i], ids_recv.at[s], ((s + i) % n_seq, v)).wait_send()
    loop(1, n_seq, ids_left)
    loop(1, n_vocab, lambda i: stat(i).wait_send())
    loop(0, chips, lambda i: sib_copy(i).wait_send())
    loop(1, chips, lambda i: share_copy((c + i) % chips).wait_send())
    for b in range(n_seq):
        @pl.when(jnp.logical_and(s >= b, s < n_seq - 1))
        def _(b=b):
            go_up(b).wait_send()

        @pl.when(jnp.logical_and(s <= b, s > 0))
        def _(b=b):
            go_down(b).wait_send()


def body(hidden, embed_cotangent, table, token_ids, target_ids, loss_scale):
    n_seq, n_vocab = lax.axis_size("seq"), lax.axis_size("vocab")
    per, chips = n_vocab // n_seq, n_vocab // CORES
    tokens, cols = hidden.shape
    vocab_rows, width = table.shape
    vmem = pl.BlockSpec(memory_space=pltpu.VMEM)
    dma = pltpu.SemaphoreType.DMA
    blocks = pltpu.VMEM((n_vocab, cols, tokens), BF16)
    halves = pltpu.VMEM((chips, tokens, cols), BF16)
    gh, gt, loss = pl.pallas_call(
        functools.partial(kernel, n_seq, n_vocab),
        out_shape=(
            jax.ShapeDtypeStruct((cols, tokens), BF16),
            jax.ShapeDtypeStruct((per, cols, vocab_rows), F32),
            jax.ShapeDtypeStruct((1, tokens), F32),
        ),
        in_specs=[vmem, vmem, pl.BlockSpec(memory_space=pl.ANY), vmem, vmem, vmem],
        out_specs=(vmem, vmem, vmem),
        scratch_shapes=[
            pltpu.VMEM((2, CHUNK, width), BF16),
            pltpu.VMEM((n_vocab, vocab_rows, cols), BF16),
            blocks, blocks, blocks,
            pltpu.VMEM((n_seq, tokens, vocab_rows), BF16),
            pltpu.VMEM((vocab_rows, tokens), F32),
            pltpu.VMEM((n_vocab, tokens, cols), BF16),
            halves, halves,
            pltpu.VMEM((tokens, cols), F32),
            pltpu.VMEM((n_vocab, 8, tokens), F32),
            pltpu.VMEM((n_seq, 8, tokens), jnp.int32),
            pltpu.VMEM((1, tokens), F32),
            pltpu.VMEM((n_seq, cols, tokens // n_seq), BF16),
            dma((2,)), dma,
            dma((3, chips)), dma((3, chips)), dma((3, n_vocab)), dma((3, 2)), dma((3, 2)),
            dma((n_seq,)), dma((n_seq,)), dma((2, n_seq)), dma((2, n_seq)),
            dma((n_vocab,)), dma((n_vocab,)), dma((n_seq,)), dma((n_seq,)),
            dma((n_seq,)), dma((n_seq,)), dma((n_seq,)),
            dma((chips,)), dma((chips,)), dma((chips,)), dma((chips,)),
        ],
        compiler_params=pltpu.CompilerParams(
            collective_id=0, has_side_effects=True, vmem_limit_bytes=62 * 1024 * 1024
        ),
        cost_estimate=pl.CostEstimate(
            flops=8 * tokens * vocab_rows * width, bytes_accessed=2 * vocab_rows * width,
            transcendentals=2 * tokens * vocab_rows,
        ),
    )(
        hidden.T, embed_cotangent.T, table,
        jnp.broadcast_to(token_ids[None, :], (8, tokens)),
        target_ids[None, :], loss_scale[None, :],
    )
    return (gh.T, gt.reshape(per * cols, vocab_rows).T, loss[0])


def solution(mesh):
    placed = (P("seq", "vocab"), P("seq", "vocab"), P("vocab", None), P("seq"), P("seq"), P("seq"))
    return jax.shard_map(
        body,
        mesh=mesh,
        in_specs=placed,
        out_specs=(P("seq", "vocab"), P("vocab", "seq"), P("seq")),
        check_vma=False,
    )
```

```python
import functools

import jax
import jax.numpy as jnp
from jax import lax
from jax.experimental import pallas as pl
from jax.experimental.pallas import tpu as pltpu
from jax.sharding import PartitionSpec as P

MESH = pl.DeviceIdType.MESH
F32 = jnp.float32
BF16 = jnp.bfloat16
CORES = 2
CHUNK = 128


def dot(a, b, dims=(((1,), (0,)), ((), ()))):
    return lax.dot_general(a, b, dims, preferred_element_type=F32)


def kernel(
    n_seq, n_vocab,
    hid, cot, table, ids, target, scale,
    gh, gt, loss,
    raw, tab, rows, hcols, ccols, grads, logits, sends, sib, shares, own, stats, ids_all, norm, stage, corner,
    table_sem, local_sem, push_sem, fwd_sem, block_sem, half_send, half_recv,
    stage_send, stage_recv, cross_send, cross_recv, stat_send, stat_recv, ids_send, ids_recv,
    up_sem, down_sem, grads_recv, sib_send, sib_recv, share_send, share_recv,
    corner_send, corner_recv, side_send, side_recv,
):
    per = n_vocab // n_seq
    chips = n_vocab // CORES
    cols, tokens = hid.shape
    vocab_rows, _ = table.shape
    s, v = lax.axis_index("seq"), lax.axis_index("vocab")
    c, k = v // CORES, v % CORES
    twin = c * CORES + (1 - k)
    q, r = v // per, v % per
    quarter = tokens // n_seq
    square = chips == 4
    nx, ny, nd = c + 1 - 2 * (c % 2), (c + 2) % 4, 3 - c
    half = cols // 2
    base = v * vocab_rows

    def remote(src, dst, send, recv, where):
        return pltpu.make_async_remote_copy(
            src_ref=src, dst_ref=dst, send_sem=send, recv_sem=recv,
            device_id=where, device_id_type=MESH,
        )

    def lanes(b):
        return pl.ds(pl.multiple_of(b * quarter, quarter), quarter)

    def loop(lo, hi, fn):
        lax.fori_loop(lo, hi, lambda i, z: (fn(i), z)[1], 0)

    def fetch(i):
        at = pl.ds(pl.multiple_of(i * CHUNK, CHUNK), CHUNK)
        return pltpu.make_async_copy(table.at[at], raw.at[i % 2], table_sem.at[i % 2])
    fetch(0).start()
    keep = pltpu.make_async_copy(hid, rows.at[v], local_sem)
    keep.start()

    barrier = pltpu.get_barrier_semaphore()
    loop(1, n_vocab, lambda i: pl.semaphore_signal(
        barrier, inc=1, device_id=(s, (v + i) % n_vocab), device_id_type=MESH))
    loop(1, n_seq, lambda i: pl.semaphore_signal(
        barrier, inc=1, device_id=((s + i) % n_seq, v), device_id_type=MESH))

    pl.semaphore_wait(barrier, n_vocab + n_seq - 2)

    def core_of(chip, core):
        return chip * CORES + core

    def peers(fn):
        if square:
            fn(1, nx)
            fn(2, ny)
        else:
            loop(1, chips, lambda i: fn(i, (c + i) % chips))

    def push_copy(a, src, buf, i, u):
        return remote(src, buf.at[v], push_sem.at[a, i], block_sem.at[a, v], (s, u))

    def push(a, src, buf):
        peers(lambda i, chip: push_copy(a, src, buf, i, core_of(chip, k)).start())
        push_copy(a, src, buf, 0, twin).start()

    def arrived(a, buf, u):
        remote(buf.at[u], buf.at[u], fwd_sem.at[a, 0], block_sem.at[a, u], (s, twin)).wait_recv()

    def forward(a, buf, i, u):
        return remote(buf.at[u], buf.at[u], fwd_sem.at[a, i], block_sem.at[a, u], (s, twin))

    def half_copy(a, buf, i, u, chip):
        part = buf.at[u, pl.ds(i * half, half), :]
        return remote(part, part, half_send.at[a, i], half_recv.at[a, i], (s, core_of(chip, k)))

    def near(a, buf):
        def one(i, chip):
            u = core_of(chip, k)
            arrived(a, buf, u)
            if square:
                half_copy(a, buf, i - 1, u, ny if i == 1 else nx).start()
            forward(a, buf, i, u).start()
        peers(one)

    def far(a, buf):
        if square:
            u = core_of(nd, k)
            half_copy(a, buf, 0, u, ny).wait_recv()
            half_copy(a, buf, 1, u, nx).wait_recv()
            forward(a, buf, 3, u).start()

    def from_twin(a, buf):
        loop(0, chips, lambda i: arrived(a, buf, core_of((c + i) % chips, 1 - k)))

    def gather_done(a, src, buf):
        peers(lambda i, chip: push_copy(a, src, buf, i, core_of(chip, k)).wait_send())
        push_copy(a, src, buf, 0, twin).wait_send()
        loop(1, chips, lambda i: forward(a, buf, i, v).wait_send())
        if square:
            half_copy(a, buf, 0, v, ny).wait_send()
            half_copy(a, buf, 1, v, nx).wait_send()

    push(0, hid, rows)

    def stage_copy(to):
        return remote(cot.at[:, lanes(to)], stage.at[q], stage_send.at[to], stage_recv.at[q],
                      (s, to * per + r))
    loop(1, n_seq, lambda j: stage_copy((q + j) % n_seq).start())
    stage[q] = cot[:, lanes(q)]

    def cross(a, j, src, buf):
        d = (s + j) % n_seq
        return remote(src(d), buf.at[v, :, lanes(s)], cross_send.at[a, j], cross_recv.at[a, s], (d, v))

    def cross_in(a, buf):
        def one(j):
            b = (s + j) % n_seq
            here = buf.at[v, :, lanes(b)]
            remote(here, here, cross_send.at[a, j], cross_recv.at[a, b], (b, v)).wait_recv()
        loop(1, n_seq, one)

    def cot_part(d):
        return stage.at[d]

    def hid_part(d):
        return rows.at[d * per + r, :, lanes(q)]

    ids_all[s] = jnp.broadcast_to(ids[...], (8, tokens))

    def ids_copy(i):
        mine = ids_all.at[s]
        return remote(mine, mine, ids_send.at[i], ids_recv.at[s], ((s + i) % n_seq, v))

    def send_ids(i):
        ids_copy(i).start()
    loop(1, n_seq, send_ids)

    pieces = vocab_rows // CHUNK

    def split(i):
        @pl.when(i + 1 < pieces)
        def _():
            fetch(i + 1).start()
        fetch(i).wait()
        at = pl.ds(pl.multiple_of(i * CHUNK, CHUNK), CHUNK)
        for u in range(n_vocab):
            tab[u, at, :] = raw[i % 2, :, u * cols:(u + 1) * cols]
    loop(0, pieces, split)

    def stage_in(j):
        b = (q + j) % n_seq
        remote(stage.at[b], stage.at[b], stage_send.at[b], stage_recv.at[b], (s, twin)).wait_recv()
    loop(1, n_seq, stage_in)
    loop(1, n_seq, lambda j: cross(1, j, cot_part, ccols).start())
    ccols[v, :, lanes(s)] = stage[s]

    logits[...] = jnp.zeros_like(logits)
    gt[...] = jnp.zeros_like(gt)
    keep.wait()

    def add_logits(u):
        logits[...] += dot(tab[u], rows[u])

    add_logits(v)
    near(0, rows)

    def step(i):
        chip = (c + i) % chips
        mine = core_of(chip, k)

        if not square:
            @pl.when(i > 0)
            def _():
                add_logits(mine)
        arrived(0, rows, core_of(chip, 1 - k))
        add_logits(core_of(chip, 1 - k))
    if square:
        def pair(i):
            chip = nx * (1 - i) + ny * i
            add_logits(core_of(chip, k))
            arrived(0, rows, core_of(chip, 1 - k))
            add_logits(core_of(chip, 1 - k))
        loop(0, 2, pair)
        far(0, rows)
        add_logits(core_of(nd, k))

    loop(1, n_seq, lambda j: cross(0, j, hid_part, hcols).start())
    hcols[v, :, lanes(s)] = rows[s * per + r, :, lanes(q)]
    cross_in(1, ccols)
    push(1, ccols.at[v], ccols)
    if square:
        def last(i):
            chip = c * (1 - i) + nd * i
            arrived(0, rows, core_of(chip, 1 - k))
            add_logits(core_of(chip, 1 - k))
        loop(0, 2, last)
    else:
        loop(0, chips, step)

    def piece(i):
        at = pl.ds(pl.multiple_of(i * CHUNK, CHUNK), CHUNK)
        entry = base + i * CHUNK + lax.broadcasted_iota(jnp.int32, (CHUNK, tokens), 0)
        return at, entry

    top = lax.fori_loop(
        0, pieces,
        lambda i, m: jnp.maximum(m, jnp.max(logits[piece(i)[0], :], axis=0, keepdims=True)),
        jnp.full((1, tokens), -jnp.inf, F32))

    def sums(i, carry):
        total, picked = carry
        at, entry = piece(i)
        x = logits[at, :]
        total += jnp.sum(jnp.exp(x - top), axis=0, keepdims=True)
        picked += jnp.sum(jnp.where(entry == target[...], x, 0.0), axis=0, keepdims=True)
        return total, picked
    zero = jnp.zeros((1, tokens), F32)
    total, picked = lax.fori_loop(0, pieces, sums, (zero, zero))
    stats[v] = jnp.concatenate([top, total, picked, jnp.zeros((5, tokens), F32)], axis=0)

    def stat(i):
        return remote(stats.at[v], stats.at[v], stat_send.at[i], stat_recv.at[v],
                      (s, (v + i) % n_vocab))
    loop(1, n_vocab, lambda i: stat(i).start())

    def stat_wait(i):
        u = (v + i) % n_vocab
        remote(stats.at[u], stats.at[u], stat_send.at[i], stat_recv.at[u], (s, twin)).wait_recv()
    loop(1, n_vocab, stat_wait)
    every = stats[...]
    row_top = jnp.max(every[:, 0, :], axis=0, keepdims=True)
    exp_total = jnp.sum(every[:, 1, :] * jnp.exp(every[:, 0, :] - row_top), axis=0, keepdims=True)
    log_norm = row_top + jnp.log(exp_total)
    loss[...] = log_norm - jnp.sum(every[:, 2, :], axis=0, keepdims=True)
    norm[...] = log_norm

    def logit_grad(i):
        at, entry = piece(i)
        hot = jnp.where(entry == target[...], 1.0, 0.0)
        g = scale[...] * (jnp.exp(logits[at, :] - norm[...]) - hot)
        grads[s, :, at] = g.T.astype(BF16)
    loop(0, pieces, logit_grad)

    def go_up(b):
        return remote(grads.at[b], grads.at[b], up_sem.at[b], grads_recv.at[b],
                      (jnp.minimum(s + 1, n_seq - 1), v))

    def go_down(b):
        return remote(grads.at[b], grads.at[b], down_sem.at[b], grads_recv.at[b],
                      (jnp.maximum(s - 1, 0), v))

    @pl.when(s < n_seq - 1)
    def _():
        go_up(s).start()

    @pl.when(s > 0)
    def _():
        go_down(s).start()

    def sib_copy(ci):
        slot = sends.at[ci * CORES + 1 - k]
        return remote(slot, sib.at[ci], sib_send.at[ci], sib_recv.at[ci], (s, twin))

    def to_twin(i):
        ci = (c + i) % chips
        u = ci * CORES + 1 - k
        sends[u] = dot(grads[s], tab[u]).astype(BF16)
        sib_copy(ci).start()
    loop(1, chips + 1, to_twin)
    near(1, ccols)
    cross_in(0, hcols)
    push(2, hcols.at[v], hcols)

    def share_copy(ci):
        slot = sends.at[ci * CORES + k]
        return remote(slot, shares.at[c], share_send.at[ci], share_recv.at[c], (s, ci * CORES + k))

    def pair_sum(ci):
        own[...] = dot(grads[s], tab[ci * CORES + k])
        sib_copy(ci).wait_recv()
        own[...] += sib[ci].astype(F32)

    def to_chips(i):
        ci = (c + i) % chips
        pair_sum(ci)

        @pl.when(i < chips)
        def _():
            sends[ci * CORES + k] = own[...].astype(BF16)
            share_copy(ci).start()

    side = tokens // 2

    def side_of(i):
        return pl.ds(i * side, side)

    def corner_copy(i):
        return remote(sends.at[nd * CORES + k, side_of(i), :], corner.at[i], corner_send.at[i],
                      corner_recv.at[i], (s, (ny if i else nx) * CORES + k))

    def side_copy(to, i):
        chip = ny if to else nx
        return remote(sends.at[chip * CORES + k, side_of(i), :], shares.at[c, side_of(i), :],
                      side_send.at[to, i], side_recv.at[to, i], (s, chip * CORES + k))

    def share_start():
        if not square:
            loop(1, chips + 1, to_chips)
            return

        def one(i):
            ci = c + (i == 0) * (nd - c) + (i == 1) * (nx - c) + (i == 2) * (ny - c)
            pair_sum(ci)

            @pl.when(i < 3)
            def _():
                sends[ci * CORES + k] = own[...].astype(BF16)
            for at, copies in enumerate(
                ((corner_copy(0), corner_copy(1)), (side_copy(0, 0),), (side_copy(1, 1),))
            ):
                @pl.when(i == at)
                def _(copies=copies):
                    for copy in copies:
                        copy.start()
        loop(0, 4, one)

    def share_pass():
        if square:
            for to in (0, 1):
                corner_copy(1 - to).wait_recv()
                u = (ny if to else nx) * CORES + k
                at = side_of(1 - to)
                sends[u, at, :] = (
                    sends[u, at, :].astype(F32) + corner[1 - to].astype(F32)
                ).astype(BF16)
                side_copy(to, 1 - to).start()

    share_start()

    def tokens_of(buf, b, j):
        return jnp.concatenate([buf[i * per + j, :, lanes(b)] for i in range(n_seq)], axis=1)

    def add_head(b):
        def one(j):
            gt[j] += dot(tokens_of(hcols, b, j), grads[b])
        loop(0, per, one)

    def take_grads(j):
        @pl.when(s >= j)
        def _():
            b = s - j
            go_up(b).wait_recv()

            @pl.when(s < n_seq - 1)
            def _():
                go_up(b).start()

        @pl.when(s + j < n_seq)
        def _():
            b = s + j
            go_down(b).wait_recv()

            @pl.when(s > 0)
            def _():
                go_down(b).start()

    def add_heads(j):
        @pl.when(s >= j)
        def _():
            add_head(s - j)

        @pl.when(s + j < n_seq)
        def _():
            add_head(s + j)

    def ids_wait(i):
        b = (s + i) % n_seq
        remote(ids_all.at[b], ids_all.at[b], ids_send.at[i], ids_recv.at[b], (b, v)).wait_recv()

    def add_embed(b):
        entry = base + lax.broadcasted_iota(jnp.int32, (vocab_rows, tokens), 0)
        hot = jnp.where(entry == ids_all[b][0:1, :], 1.0, 0.0).astype(BF16)

        def one(j):
            gt[j] += dot(tokens_of(ccols, b, j), hot, (((1,), (1,)), ((), ())))
        loop(0, per, one)

    take_grads(1)
    far(1, ccols)
    near(2, hcols)
    share_pass()
    loop(1, n_seq, ids_wait)
    from_twin(1, ccols)
    loop(0, n_seq, add_embed)
    if n_seq > 2:
        take_grads(2)
    far(2, hcols)
    from_twin(2, hcols)
    add_head(s)
    add_heads(1)
    for j in range(2, n_seq):
        if j > 2:
            take_grads(j)
        add_heads(j)

    def share_add(ci):
        own[...] += shares[ci].astype(F32)

    def share_in(i):
        ci = (c + i) % chips
        remote(shares.at[ci], shares.at[ci], share_send.at[ci], share_recv.at[ci],
               (s, twin)).wait_recv()
        share_add(ci)
    if square:
        for to in (0, 1):
            side_copy(to, 0).wait_recv()
            side_copy(to, 1).wait_recv()
            share_add(ny if to else nx)
    else:
        loop(1, chips, share_in)
    gh[...] = own[...].T.astype(BF16)

    gather_done(0, hid, rows)
    gather_done(1, ccols.at[v], ccols)
    gather_done(2, hcols.at[v], hcols)
    loop(1, n_seq, lambda j: stage_copy((q + j) % n_seq).wait_send())
    loop(1, n_seq, lambda j: cross(0, j, hid_part, hcols).wait_send())
    loop(1, n_seq, lambda j: cross(1, j, cot_part, ccols).wait_send())

    def ids_left(i):
        ids_copy(i).wait_send()
    loop(1, n_seq, ids_left)
    loop(1, n_vocab, lambda i: stat(i).wait_send())
    loop(0, chips, lambda i: sib_copy(i).wait_send())
    if square:
        for i in (0, 1):
            corner_copy(i).wait_send()
            side_copy(0, i).wait_send()
            side_copy(1, i).wait_send()
    else:
        loop(1, chips, lambda i: share_copy((c + i) % chips).wait_send())
    for b in range(n_seq):
        @pl.when(jnp.logical_and(s >= b, s < n_seq - 1))
        def _(b=b):
            go_up(b).wait_send()

        @pl.when(jnp.logical_and(s <= b, s > 0))
        def _(b=b):
            go_down(b).wait_send()


def body(hidden, embed_cotangent, table, token_ids, target_ids, loss_scale):
    n_seq, n_vocab = lax.axis_size("seq"), lax.axis_size("vocab")
    per, chips = n_vocab // n_seq, n_vocab // CORES
    tokens, cols = hidden.shape
    vocab_rows, width = table.shape
    vmem = pl.BlockSpec(memory_space=pltpu.VMEM)
    dma = pltpu.SemaphoreType.DMA
    blocks = pltpu.VMEM((n_vocab, cols, tokens), BF16)
    halves = pltpu.VMEM((chips, tokens, cols), BF16)
    gh, gt, loss = pl.pallas_call(
        functools.partial(kernel, n_seq, n_vocab),
        out_shape=(
            jax.ShapeDtypeStruct((cols, tokens), BF16),
            jax.ShapeDtypeStruct((per, cols, vocab_rows), F32),
            jax.ShapeDtypeStruct((1, tokens), F32),
        ),
        in_specs=[vmem, vmem, pl.BlockSpec(memory_space=pl.ANY), vmem, vmem, vmem],
        out_specs=(vmem, vmem, vmem),
        scratch_shapes=[
            pltpu.VMEM((2, CHUNK, width), BF16),
            pltpu.VMEM((n_vocab, vocab_rows, cols), BF16),
            blocks, blocks, blocks,
            pltpu.VMEM((n_seq, tokens, vocab_rows), BF16),
            pltpu.VMEM((vocab_rows, tokens), F32),
            pltpu.VMEM((n_vocab, tokens, cols), BF16),
            halves, halves,
            pltpu.VMEM((tokens, cols), F32),
            pltpu.VMEM((n_vocab, 8, tokens), F32),
            pltpu.VMEM((n_seq, 8, tokens), jnp.int32),
            pltpu.VMEM((1, tokens), F32),
            pltpu.VMEM((n_seq, cols, tokens // n_seq), BF16),
            pltpu.VMEM((2, tokens // 2, cols), BF16),
            dma((2,)), dma,
            dma((3, chips)), dma((3, chips)), dma((3, n_vocab)), dma((3, 2)), dma((3, 2)),
            dma((n_seq,)), dma((n_seq,)), dma((2, n_seq)), dma((2, n_seq)),
            dma((n_vocab,)), dma((n_vocab,)), dma((n_seq,)), dma((n_seq,)),
            dma((n_seq,)), dma((n_seq,)), dma((n_seq,)),
            dma((chips,)), dma((chips,)), dma((chips,)), dma((chips,)),
            dma((2,)), dma((2,)), dma((2, 2)), dma((2, 2)),
        ],
        compiler_params=pltpu.CompilerParams(
            collective_id=0, has_side_effects=True, vmem_limit_bytes=62 * 1024 * 1024
        ),
        cost_estimate=pl.CostEstimate(
            flops=8 * tokens * vocab_rows * width, bytes_accessed=2 * vocab_rows * width,
            transcendentals=2 * tokens * vocab_rows,
        ),
    )(
        hidden.T, embed_cotangent.T, table,
        token_ids[None, :], target_ids[None, :], loss_scale[None, :],
    )
    return (gh.T, gt.reshape(per * cols, vocab_rows).T, loss[0])


def solution(mesh):
    placed = (P("seq", "vocab"), P("seq", "vocab"), P("vocab", None), P("seq"), P("seq"), P("seq"))
    return jax.shard_map(
        body,
        mesh=mesh,
        in_specs=placed,
        out_specs=(P("seq", "vocab"), P("vocab", "seq"), P("seq")),
        check_vma=False,
    )
```

```python
import functools

import jax
import jax.numpy as jnp
from jax import lax
from jax.experimental import pallas as pl
from jax.experimental.pallas import tpu as pltpu
from jax.sharding import PartitionSpec as P

MESH = pl.DeviceIdType.MESH
F32 = jnp.float32
BF16 = jnp.bfloat16
CORES = 2
CHUNK = 128


def dot(a, b, dims=(((1,), (0,)), ((), ()))):
    return lax.dot_general(a, b, dims, preferred_element_type=F32)


def kernel(
    n_seq, n_vocab,
    hid, cot, table, ids, target, scale,
    gh, gt, loss,
    raw, tab, rows, hcols, ccols, grads, logits, sends, sib, shares, own, stats, ids_all, norm, stage, corner,
    table_sem, local_sem, push_sem, fwd_sem, block_sem, half_send, half_recv,
    stage_send, stage_recv, cross_send, cross_recv, stat_send, stat_recv, ids_send, ids_recv,
    up_sem, down_sem, grads_recv, sib_send, sib_recv, share_send, share_recv,
    corner_send, corner_recv, side_send, side_recv,
):
    per = n_vocab // n_seq
    chips = n_vocab // CORES
    cols, tokens = hid.shape
    vocab_rows, _ = table.shape
    s, v = lax.axis_index("seq"), lax.axis_index("vocab")
    c, k = v // CORES, v % CORES
    twin = c * CORES + (1 - k)
    q, r = v // per, v % per
    quarter = tokens // n_seq
    square = chips == 4
    nx, ny, nd = c + 1 - 2 * (c % 2), (c + 2) % 4, 3 - c
    half = cols // 2
    base = v * vocab_rows

    def remote(src, dst, send, recv, where):
        return pltpu.make_async_remote_copy(
            src_ref=src, dst_ref=dst, send_sem=send, recv_sem=recv,
            device_id=where, device_id_type=MESH,
        )

    def lanes(b):
        return pl.ds(pl.multiple_of(b * quarter, quarter), quarter)

    def loop(lo, hi, fn):
        lax.fori_loop(lo, hi, lambda i, z: (fn(i), z)[1], 0)

    def fetch(i):
        at = pl.ds(pl.multiple_of(i * CHUNK, CHUNK), CHUNK)
        return pltpu.make_async_copy(table.at[at], raw.at[i % 2], table_sem.at[i % 2])
    fetch(0).start()
    keep = pltpu.make_async_copy(hid, rows.at[v], local_sem)
    keep.start()

    barrier = pltpu.get_barrier_semaphore()
    loop(1, n_vocab, lambda i: pl.semaphore_signal(
        barrier, inc=1, device_id=(s, (v + i) % n_vocab), device_id_type=MESH))
    loop(1, n_seq, lambda i: pl.semaphore_signal(
        barrier, inc=1, device_id=((s + i) % n_seq, v), device_id_type=MESH))

    pl.semaphore_wait(barrier, n_vocab + n_seq - 2)

    def core_of(chip, core):
        return chip * CORES + core

    def peers(fn):
        if square:
            fn(1, nx)
            fn(2, ny)
        else:
            loop(1, chips, lambda i: fn(i, (c + i) % chips))

    def push_copy(a, src, buf, i, u):
        return remote(src, buf.at[v], push_sem.at[a, i], block_sem.at[a, v], (s, u))

    def push(a, src, buf):
        peers(lambda i, chip: push_copy(a, src, buf, i, core_of(chip, k)).start())
        push_copy(a, src, buf, 0, twin).start()

    def arrived(a, buf, u):
        remote(buf.at[u], buf.at[u], fwd_sem.at[a, 0], block_sem.at[a, u], (s, twin)).wait_recv()

    def forward(a, buf, i, u):
        return remote(buf.at[u], buf.at[u], fwd_sem.at[a, i], block_sem.at[a, u], (s, twin))

    def half_copy(a, buf, i, u, chip):
        part = buf.at[u, pl.ds(i * half, half), :]
        return remote(part, part, half_send.at[a, i], half_recv.at[a, i], (s, core_of(chip, k)))

    def near(a, buf):
        def one(i, chip):
            u = core_of(chip, k)
            arrived(a, buf, u)
            if square:
                half_copy(a, buf, i - 1, u, ny if i == 1 else nx).start()
            forward(a, buf, i, u).start()
        peers(one)

    def far(a, buf):
        if square:
            u = core_of(nd, k)
            half_copy(a, buf, 0, u, ny).wait_recv()
            half_copy(a, buf, 1, u, nx).wait_recv()
            forward(a, buf, 3, u).start()

    def from_twin(a, buf):
        loop(0, chips, lambda i: arrived(a, buf, core_of((c + i) % chips, 1 - k)))

    def gather_done(a, src, buf):
        peers(lambda i, chip: push_copy(a, src, buf, i, core_of(chip, k)).wait_send())
        push_copy(a, src, buf, 0, twin).wait_send()
        loop(1, chips, lambda i: forward(a, buf, i, v).wait_send())
        if square:
            half_copy(a, buf, 0, v, ny).wait_send()
            half_copy(a, buf, 1, v, nx).wait_send()

    push(0, hid, rows)

    def stage_copy(to):
        return remote(cot.at[:, lanes(to)], stage.at[q], stage_send.at[to], stage_recv.at[q],
                      (s, to * per + r))
    loop(1, n_seq, lambda j: stage_copy((q + j) % n_seq).start())
    stage[q] = cot[:, lanes(q)]

    def cross(a, j, src, buf):
        d = (s + j) % n_seq
        return remote(src(d), buf.at[v, :, lanes(s)], cross_send.at[a, j], cross_recv.at[a, s], (d, v))

    def cross_in(a, buf):
        def one(j):
            b = (s + j) % n_seq
            here = buf.at[v, :, lanes(b)]
            remote(here, here, cross_send.at[a, j], cross_recv.at[a, b], (b, v)).wait_recv()
        loop(1, n_seq, one)

    def cot_part(d):
        return stage.at[d]

    def hid_part(d):
        return rows.at[d * per + r, :, lanes(q)]

    ids_all[s] = jnp.broadcast_to(ids[...], (8, tokens))

    def ids_copy(i):
        mine = ids_all.at[s]
        return remote(mine, mine, ids_send.at[i], ids_recv.at[s], ((s + i) % n_seq, v))

    def send_ids(i):
        ids_copy(i).start()
    loop(1, n_seq, send_ids)

    pieces = vocab_rows // CHUNK

    def split(i):
        @pl.when(i + 1 < pieces)
        def _():
            fetch(i + 1).start()
        fetch(i).wait()
        at = pl.ds(pl.multiple_of(i * CHUNK, CHUNK), CHUNK)
        for u in range(n_vocab):
            tab[u, at, :] = raw[i % 2, :, u * cols:(u + 1) * cols]
    loop(0, pieces, split)

    logits[...] = jnp.zeros_like(logits)
    gt[...] = jnp.zeros_like(gt)
    keep.wait()

    def add_logits(u):
        logits[...] += dot(tab[u], rows[u])

    add_logits(v)
    near(0, rows)

    def stage_in(j):
        b = (q + j) % n_seq
        remote(stage.at[b], stage.at[b], stage_send.at[b], stage_recv.at[b], (s, twin)).wait_recv()
    loop(1, n_seq, stage_in)
    loop(1, n_seq, lambda j: cross(1, j, cot_part, ccols).start())
    ccols[v, :, lanes(s)] = stage[s]

    def step(i):
        chip = (c + i) % chips
        mine = core_of(chip, k)

        if not square:
            @pl.when(i > 0)
            def _():
                add_logits(mine)
        arrived(0, rows, core_of(chip, 1 - k))
        add_logits(core_of(chip, 1 - k))
    if square:
        def pair(i):
            chip = nx * (1 - i) + ny * i
            add_logits(core_of(chip, k))
            arrived(0, rows, core_of(chip, 1 - k))
            add_logits(core_of(chip, 1 - k))
        loop(0, 2, pair)
        far(0, rows)
        add_logits(core_of(nd, k))

    loop(1, n_seq, lambda j: cross(0, j, hid_part, hcols).start())
    hcols[v, :, lanes(s)] = rows[s * per + r, :, lanes(q)]
    cross_in(1, ccols)
    push(1, ccols.at[v], ccols)
    if square:
        def last(i):
            chip = c * (1 - i) + nd * i
            arrived(0, rows, core_of(chip, 1 - k))
            add_logits(core_of(chip, 1 - k))
        loop(0, 2, last)
    else:
        loop(0, chips, step)

    def piece(i):
        at = pl.ds(pl.multiple_of(i * CHUNK, CHUNK), CHUNK)
        entry = base + i * CHUNK + lax.broadcasted_iota(jnp.int32, (CHUNK, tokens), 0)
        return at, entry

    top = lax.fori_loop(
        0, pieces,
        lambda i, m: jnp.maximum(m, jnp.max(logits[piece(i)[0], :], axis=0, keepdims=True)),
        jnp.full((1, tokens), -jnp.inf, F32))

    def sums(i, carry):
        total, picked = carry
        at, entry = piece(i)
        x = logits[at, :]
        total += jnp.sum(jnp.exp(x - top), axis=0, keepdims=True)
        picked += jnp.sum(jnp.where(entry == target[...], x, 0.0), axis=0, keepdims=True)
        return total, picked
    zero = jnp.zeros((1, tokens), F32)
    total, picked = lax.fori_loop(0, pieces, sums, (zero, zero))
    stats[v] = jnp.concatenate([top, total, picked, jnp.zeros((5, tokens), F32)], axis=0)

    def stat(i):
        return remote(stats.at[v], stats.at[v], stat_send.at[i], stat_recv.at[v],
                      (s, (v + i) % n_vocab))
    loop(1, n_vocab, lambda i: stat(i).start())

    def stat_wait(i):
        u = (v + i) % n_vocab
        remote(stats.at[u], stats.at[u], stat_send.at[i], stat_recv.at[u], (s, twin)).wait_recv()
    loop(1, n_vocab, stat_wait)
    every = stats[...]
    row_top = jnp.max(every[:, 0, :], axis=0, keepdims=True)
    exp_total = jnp.sum(every[:, 1, :] * jnp.exp(every[:, 0, :] - row_top), axis=0, keepdims=True)
    log_norm = row_top + jnp.log(exp_total)
    loss[...] = log_norm - jnp.sum(every[:, 2, :], axis=0, keepdims=True)
    norm[...] = log_norm

    def logit_grad(i):
        at, entry = piece(i)
        hot = jnp.where(entry == target[...], 1.0, 0.0)
        g = scale[...] * (jnp.exp(logits[at, :] - norm[...]) - hot)
        grads[s, :, at] = g.T.astype(BF16)
    loop(0, pieces, logit_grad)

    def go_up(b):
        return remote(grads.at[b], grads.at[b], up_sem.at[b], grads_recv.at[b],
                      (jnp.minimum(s + 1, n_seq - 1), v))

    def go_down(b):
        return remote(grads.at[b], grads.at[b], down_sem.at[b], grads_recv.at[b],
                      (jnp.maximum(s - 1, 0), v))

    @pl.when(s < n_seq - 1)
    def _():
        go_up(s).start()

    @pl.when(s > 0)
    def _():
        go_down(s).start()

    def sib_copy(ci):
        slot = sends.at[ci * CORES + 1 - k]
        return remote(slot, sib.at[ci], sib_send.at[ci], sib_recv.at[ci], (s, twin))

    cross_in(0, hcols)
    push(2, hcols.at[v], hcols)

    def to_twin(i):
        ci = (c + i) % chips
        u = ci * CORES + 1 - k
        sends[u] = dot(grads[s], tab[u]).astype(BF16)
        sib_copy(ci).start()
    loop(1, chips + 1, to_twin)
    near(1, ccols)

    def share_copy(ci):
        slot = sends.at[ci * CORES + k]
        return remote(slot, shares.at[c], share_send.at[ci], share_recv.at[c], (s, ci * CORES + k))

    def pair_sum(ci):
        own[...] = dot(grads[s], tab[ci * CORES + k])
        sib_copy(ci).wait_recv()
        own[...] += sib[ci].astype(F32)

    def to_chips(i):
        ci = (c + i) % chips
        pair_sum(ci)

        @pl.when(i < chips)
        def _():
            sends[ci * CORES + k] = own[...].astype(BF16)
            share_copy(ci).start()

    side = tokens // 2

    def side_of(i):
        return pl.ds(i * side, side)

    def corner_copy(i):
        return remote(sends.at[nd * CORES + k, side_of(i), :], corner.at[i], corner_send.at[i],
                      corner_recv.at[i], (s, (ny if i else nx) * CORES + k))

    def side_copy(to, i):
        chip = ny if to else nx
        return remote(sends.at[chip * CORES + k, side_of(i), :], shares.at[c, side_of(i), :],
                      side_send.at[to, i], side_recv.at[to, i], (s, chip * CORES + k))

    def share_start():
        if not square:
            loop(1, chips + 1, to_chips)
            return

        def one(i):
            ci = c + (i == 0) * (nd - c) + (i == 1) * (nx - c) + (i == 2) * (ny - c)
            pair_sum(ci)

            @pl.when(i < 3)
            def _():
                sends[ci * CORES + k] = own[...].astype(BF16)
            for at, copies in enumerate(
                ((corner_copy(0), corner_copy(1)), (side_copy(0, 0),), (side_copy(1, 1),))
            ):
                @pl.when(i == at)
                def _(copies=copies):
                    for copy in copies:
                        copy.start()
        loop(0, 4, one)

    def share_pass():
        if square:
            for to in (0, 1):
                corner_copy(1 - to).wait_recv()
                u = (ny if to else nx) * CORES + k
                at = side_of(1 - to)
                sends[u, at, :] = (
                    sends[u, at, :].astype(F32) + corner[1 - to].astype(F32)
                ).astype(BF16)
                side_copy(to, 1 - to).start()

    share_start()

    def tokens_of(buf, b, j):
        return jnp.concatenate([buf[i * per + j, :, lanes(b)] for i in range(n_seq)], axis=1)

    def add_head(b):
        def one(j):
            gt[j] += dot(tokens_of(hcols, b, j), grads[b])
        loop(0, per, one)

    def take_grads(j):
        @pl.when(s >= j)
        def _():
            b = s - j
            go_up(b).wait_recv()

            @pl.when(s < n_seq - 1)
            def _():
                go_up(b).start()

        @pl.when(s + j < n_seq)
        def _():
            b = s + j
            go_down(b).wait_recv()

            @pl.when(s > 0)
            def _():
                go_down(b).start()

    def add_heads(j):
        @pl.when(s >= j)
        def _():
            add_head(s - j)

        @pl.when(s + j < n_seq)
        def _():
            add_head(s + j)

    def ids_wait(i):
        b = (s + i) % n_seq
        remote(ids_all.at[b], ids_all.at[b], ids_send.at[i], ids_recv.at[b], (b, v)).wait_recv()

    def add_embed(b):
        entry = base + lax.broadcasted_iota(jnp.int32, (vocab_rows, tokens), 0)
        hot = jnp.where(entry == ids_all[b][0:1, :], 1.0, 0.0).astype(BF16)

        def one(j):
            gt[j] += dot(tokens_of(ccols, b, j), hot, (((1,), (1,)), ((), ())))
        loop(0, per, one)

    take_grads(1)
    near(2, hcols)
    far(1, ccols)
    if n_seq > 2:
        take_grads(2)
    share_pass()
    far(2, hcols)
    loop(1, n_seq, ids_wait)
    from_twin(1, ccols)
    loop(0, n_seq, add_embed)
    from_twin(2, hcols)
    add_head(s)
    add_heads(1)
    for j in range(2, n_seq):
        if j > 2:
            take_grads(j)
        add_heads(j)

    def share_add(ci):
        own[...] += shares[ci].astype(F32)

    def share_in(i):
        ci = (c + i) % chips
        remote(shares.at[ci], shares.at[ci], share_send.at[ci], share_recv.at[ci],
               (s, twin)).wait_recv()
        share_add(ci)
    if square:
        for to in (0, 1):
            side_copy(to, 0).wait_recv()
            side_copy(to, 1).wait_recv()
            share_add(ny if to else nx)
    else:
        loop(1, chips, share_in)
    gh[...] = own[...].T.astype(BF16)

    gather_done(0, hid, rows)
    gather_done(1, ccols.at[v], ccols)
    gather_done(2, hcols.at[v], hcols)
    loop(1, n_seq, lambda j: stage_copy((q + j) % n_seq).wait_send())
    loop(1, n_seq, lambda j: cross(0, j, hid_part, hcols).wait_send())
    loop(1, n_seq, lambda j: cross(1, j, cot_part, ccols).wait_send())

    def ids_left(i):
        ids_copy(i).wait_send()
    loop(1, n_seq, ids_left)
    loop(1, n_vocab, lambda i: stat(i).wait_send())
    loop(0, chips, lambda i: sib_copy(i).wait_send())
    if square:
        for i in (0, 1):
            corner_copy(i).wait_send()
            side_copy(0, i).wait_send()
            side_copy(1, i).wait_send()
    else:
        loop(1, chips, lambda i: share_copy((c + i) % chips).wait_send())
    for b in range(n_seq):
        @pl.when(jnp.logical_and(s >= b, s < n_seq - 1))
        def _(b=b):
            go_up(b).wait_send()

        @pl.when(jnp.logical_and(s <= b, s > 0))
        def _(b=b):
            go_down(b).wait_send()


def body(hidden, embed_cotangent, table, token_ids, target_ids, loss_scale):
    n_seq, n_vocab = lax.axis_size("seq"), lax.axis_size("vocab")
    per, chips = n_vocab // n_seq, n_vocab // CORES
    tokens, cols = hidden.shape
    vocab_rows, width = table.shape
    vmem = pl.BlockSpec(memory_space=pltpu.VMEM)
    dma = pltpu.SemaphoreType.DMA
    blocks = pltpu.VMEM((n_vocab, cols, tokens), BF16)
    halves = pltpu.VMEM((chips, tokens, cols), BF16)
    gh, gt, loss = pl.pallas_call(
        functools.partial(kernel, n_seq, n_vocab),
        out_shape=(
            jax.ShapeDtypeStruct((cols, tokens), BF16),
            jax.ShapeDtypeStruct((per, cols, vocab_rows), F32),
            jax.ShapeDtypeStruct((1, tokens), F32),
        ),
        in_specs=[vmem, vmem, pl.BlockSpec(memory_space=pl.ANY), vmem, vmem, vmem],
        out_specs=(vmem, vmem, vmem),
        scratch_shapes=[
            pltpu.VMEM((2, CHUNK, width), BF16),
            pltpu.VMEM((n_vocab, vocab_rows, cols), BF16),
            blocks, blocks, blocks,
            pltpu.VMEM((n_seq, tokens, vocab_rows), BF16),
            pltpu.VMEM((vocab_rows, tokens), F32),
            pltpu.VMEM((n_vocab, tokens, cols), BF16),
            halves, halves,
            pltpu.VMEM((tokens, cols), F32),
            pltpu.VMEM((n_vocab, 8, tokens), F32),
            pltpu.VMEM((n_seq, 8, tokens), jnp.int32),
            pltpu.VMEM((1, tokens), F32),
            pltpu.VMEM((n_seq, cols, tokens // n_seq), BF16),
            pltpu.VMEM((2, tokens // 2, cols), BF16),
            dma((2,)), dma,
            dma((3, chips)), dma((3, chips)), dma((3, n_vocab)), dma((3, 2)), dma((3, 2)),
            dma((n_seq,)), dma((n_seq,)), dma((2, n_seq)), dma((2, n_seq)),
            dma((n_vocab,)), dma((n_vocab,)), dma((n_seq,)), dma((n_seq,)),
            dma((n_seq,)), dma((n_seq,)), dma((n_seq,)),
            dma((chips,)), dma((chips,)), dma((chips,)), dma((chips,)),
            dma((2,)), dma((2,)), dma((2, 2)), dma((2, 2)),
        ],
        compiler_params=pltpu.CompilerParams(
            collective_id=0, has_side_effects=True, vmem_limit_bytes=62 * 1024 * 1024
        ),
        cost_estimate=pl.CostEstimate(
            flops=8 * tokens * vocab_rows * width, bytes_accessed=2 * vocab_rows * width,
            transcendentals=2 * tokens * vocab_rows,
        ),
    )(
        hidden.T, embed_cotangent.T, table,
        token_ids[None, :], target_ids[None, :], loss_scale[None, :],
    )
    return (gh.T, gt.reshape(per * cols, vocab_rows).T, loss[0])


def solution(mesh):
    placed = (P("seq", "vocab"), P("seq", "vocab"), P("vocab", None), P("seq"), P("seq"), P("seq"))
    return jax.shard_map(
        body,
        mesh=mesh,
        in_specs=placed,
        out_specs=(P("seq", "vocab"), P("vocab", "seq"), P("seq")),
        check_vma=False,
    )
```
